32 devices in a mesh: groups: 2 (over y), pool: 4 (over z), mp: 4 (over x, core).
Axes of the slice: x: 2, y: 2, z: 4, core: 2. Of those that a mesh axis runs over, the one named last changes fastest.
Arguments:
- hidden_states: bfloat16 [128, 8192], P(('groups', 'pool'), 'mp'), parts along dimension 0, may hold values from -6 to 6
- dropout_masks: int32 [8, 128, 8192], P(None, 'groups', 'mp'), parts along dimension 1, may hold values 0 or 1
- gate_weight: bfloat16 [8192, 14784], P('mp', 'pool'), may hold values from -0.0625 to 0.0625
- up_weight: bfloat16 [8192, 14784], P('mp', 'pool'), may hold values from -0.0625 to 0.0625
Outputs:
- activated: bfloat16 [8, 128, 14784], P(None, ('groups', 'mp'), 'pool'), parts along dimension 1
The draws below stay inside these ranges and needn't reach their ends.
There are 2 independent parts, one for each index of `groups`. The reference program is written for one: setup_inputs(seed, part) draws one part's arguments, and reference() takes and returns one part's arrays. A program takes and returns all parts, laid end to end along the dimension named above; an argument that names none is the same for every part. Nothing has to cross between parts.
All inputs are finite; a program needn't handle non-finite values. No bound on the sum of `dropout_masks` on one device may be relied on, other than what follows from the above.
Results may differ from the reference program's by a relative error of at most 0.015.
Values may be sent and summed in bfloat16 or wider, within the bound.
No kernel may reach another device: no remote copies, remote signals or barrier semaphores. Data moves between devices by JAX's collectives and lax.ppermute only.
A program may use at most 128 MiB of HBM per device.

```python
import jax
import jax.numpy as jnp
from jax import lax

D = 8192
FF = 14784
MASKS = 8
TOKENS = 64
N_MP = 4


def touch_ends(values, stream_key, low, top_value):
    longest = values.shape.index(max(values.shape))
    spots = []
    for shift in (0, 1):
        where = [jax.random.randint(jax.random.fold_in(stream_key, axis), (), 0, length) for axis, length in enumerate(values.shape)]
        where[longest] = (where[longest] + shift) % values.shape[longest]
        spots.append(tuple(where))
    return values.at[spots[0]].set(low).at[spots[1]].set(top_value)


def steps_of(stream_key, shape, shards, least, top_value):
    def one(axis_at, blocks):
        heights = jax.random.uniform(jax.random.fold_in(jax.random.fold_in(stream_key, 6), axis_at), (blocks,), jnp.float32, least / len(shards), top_value / len(shards))
        return jnp.repeat(jnp.exp(heights), shape[axis_at] // blocks).reshape((-1,) + (1,) * (len(shape) - axis_at - 1))

    loudness = one(*shards[0])
    for cut in shards[1:]:
        loudness = loudness * one(*cut)
    return loudness


def noise(key, dims, deviation, bound, pieces=(), dtype=jnp.bfloat16):
    array = jax.random.normal(key, dims, jnp.float32) * deviation
    if len(pieces) > 0:
        array = steps_of(key, dims, pieces, -0.22, 0.18) * array
    return jnp.clip(array, min=-bound, max=bound).astype(dtype)


def setup_inputs(seed: int = 0, part: int = 0) -> dict:
    arg_keys = jax.random.split(jax.random.key(seed), 5)
    part_keys = jax.random.split(jax.random.fold_in(arg_keys[4], part), 5)
    hidden_states = noise(part_keys[0], (TOKENS, D), 1.0, 6.0, ((0, 4), (1, 4)))
    dropout_masks = touch_ends((jax.random.randint(part_keys[1], (MASKS, TOKENS, D), 0, 10) < 9).astype(jnp.int32), jax.random.fold_in(part_keys[1], 1), 0, 1)
    gate_weight = noise(arg_keys[2], (D, FF), D ** -0.5, 0.0625, ((0, 4), (1, 4)))
    up_weight = noise(arg_keys[3], (D, FF), D ** -0.5, 0.0625, ((0, 4), (1, 4)))
    return {"hidden_states": hidden_states, "dropout_masks": dropout_masks, "gate_weight": gate_weight, "up_weight": up_weight}


def reference(hidden_states, dropout_masks, gate_weight, up_weight):
    block = D // N_MP

    def one_sample(mask_rows):
        masked = (hidden_states.astype(jnp.float32) * mask_rows.astype(jnp.float32) * (1.0 / 0.9)).astype(jnp.bfloat16)
        gate = jnp.zeros((masked.shape[0], FF), jnp.float32)
        up = jnp.zeros((masked.shape[0], FF), jnp.float32)
        for index in range(N_MP):
            rows = masked[:, index * block:(index + 1) * block]
            part_gate = jnp.dot(rows, gate_weight[index * block:(index + 1) * block], preferred_element_type=jnp.float32).astype(jnp.bfloat16)
            part_up = jnp.dot(rows, up_weight[index * block:(index + 1) * block], preferred_element_type=jnp.float32).astype(jnp.bfloat16)
            part_gate, part_up = lax.optimization_barrier((part_gate, part_up))
            gate = gate + part_gate.astype(jnp.float32)
            up = up + part_up.astype(jnp.float32)
        return (jax.nn.silu(gate) * up).astype(jnp.bfloat16)

    return lax.map(one_sample, dropout_masks)
```

```python
import functools

import jax
import jax.numpy as jnp
from jax import lax
from jax.experimental import pallas as pl
from jax.experimental.pallas import tpu as pltpu
from jax.sharding import PartitionSpec as P

BLOCK = 640
SUB = 320
COST = 1000
MIB = 2**20
NT = (((1,), (1,)), ((), ()))


def flags_kernel(dest_ref, masks_ref, flags_ref):
    del dest_ref
    flags_ref[0] = masks_ref[...].astype(jnp.float32).astype(jnp.bfloat16)


def make_flags(dest, masks, n_mp):
    samples, tokens, width = masks.shape
    rows = tokens // n_mp
    return pl.pallas_call(
        flags_kernel,
        grid_spec=pltpu.PrefetchScalarGridSpec(
            num_scalar_prefetch=1,
            grid=(n_mp,),
            in_specs=[pl.BlockSpec((samples, rows, width), lambda r, dest: (0, dest[r], 0))],
            out_specs=pl.BlockSpec((1, samples, rows, width), lambda r, dest: (r, 0, 0, 0)),
        ),
        out_shape=jax.ShapeDtypeStruct((n_mp, samples, rows, width), jnp.bfloat16),
        compiler_params=pltpu.CompilerParams(vmem_limit_bytes=16 * MIB),
        cost_estimate=pl.CostEstimate(flops=COST, bytes_accessed=COST, transcendentals=0),
        name="flags",
    )(dest, masks)


def mask_kernel(dest_ref, place_ref, flags_ref, *refs):
    hidden_refs, masked_ref, scaled = refs[:-2], refs[-2], refs[-1]
    n_pool, piece, _ = scaled.shape
    n_mp, samples, rows, _ = flags_ref.shape
    for d in range(n_pool):
        scaled[d] = hidden_refs[d][...].astype(jnp.float32) * (1.0 / 0.9)
    step = min(rows, piece)
    for r in range(n_mp):
        for low in range(0, rows, step):
            token = dest_ref[r] * rows + low
            slot = lax.rem(place_ref[0] + n_pool - lax.div(token, piece), n_pool)
            inside = pl.multiple_of(lax.rem(token, piece), step)
            part = scaled[slot, pl.ds(inside, step)]
            for m in range(samples):
                flags = flags_ref[r, m, low : low + step].astype(jnp.float32)
                masked_ref[r, m, low : low + step] = (part * flags).astype(jnp.bfloat16)


def make_masked(dest, place, flags, hiddens):
    n_mp, samples, rows, width = flags.shape
    smem = pl.BlockSpec(memory_space=pltpu.SMEM)
    vmem = pl.BlockSpec(memory_space=pltpu.VMEM)
    out = pl.pallas_call(
        mask_kernel,
        in_specs=[smem, smem, vmem] + [vmem] * len(hiddens),
        out_specs=vmem,
        out_shape=jax.ShapeDtypeStruct(flags.shape, jnp.bfloat16),
        scratch_shapes=[pltpu.VMEM((len(hiddens), *hiddens[0].shape), jnp.float32)],
        compiler_params=pltpu.CompilerParams(vmem_limit_bytes=24 * MIB),
        cost_estimate=pl.CostEstimate(flops=COST, bytes_accessed=COST, transcendentals=0),
        name="masked",
    )(dest, place, flags, *hiddens)
    return out.reshape(n_mp * samples * rows, width)


def project_kernel(start, size, masked_ref, gate_ref, up_ref, send_ref, keep_ref, held, sems):
    half = send_ref.shape[2]
    pieces = []
    for low in range(0, size, SUB):
        for which, ref in enumerate((gate_ref, up_ref)):
            n = min(SUB, size - low)
            copy = pltpu.make_async_copy(
                ref.at[pl.ds(start + low, n)], held.at[which, pl.ds(low, n)], sems.at[len(pieces)]
            )
            copy.start()
            pieces.append((which, low, n, copy))
    for which, low, n, copy in pieces:
        copy.wait()
        terms = lax.dot_general(
            held[which, low : low + n], masked_ref[...], NT, preferred_element_type=jnp.float32
        )
        send_ref[which, low : low + n] = terms[:, :half].astype(jnp.bfloat16)
        keep_ref[which, low : low + n] = terms[:, half:].astype(jnp.bfloat16)


def project(masked, gate_t, up_t, start, size):
    rows, width = masked.shape
    out = jax.ShapeDtypeStruct((2, size, rows // 2), jnp.bfloat16)
    return pl.pallas_call(
        functools.partial(project_kernel, start, size),
        in_specs=[pl.BlockSpec(memory_space=pltpu.VMEM)] + [pl.BlockSpec(memory_space=pltpu.HBM)] * 2,
        out_specs=[pl.BlockSpec(memory_space=pltpu.VMEM)] * 2,
        out_shape=[out, out],
        scratch_shapes=[
            pltpu.VMEM((2, size, width), jnp.bfloat16),
            pltpu.SemaphoreType.DMA((2 * pl.cdiv(size, SUB),)),
        ],
        compiler_params=pltpu.CompilerParams(vmem_limit_bytes=50 * MIB),
        cost_estimate=pl.CostEstimate(flops=COST, bytes_accessed=COST, transcendentals=0),
        name=f"project_{start}",
    )(masked, gate_t, up_t)


def swiglu_kernel(n_far, *refs):
    keep_ref, recv_ref, *rest = refs
    far_refs, out_ref = rest[:n_far], rest[-1]
    sums = []
    for which in range(2):
        total = keep_ref[which].astype(jnp.float32) + recv_ref[which].astype(jnp.float32)
        for far in far_refs:
            total = total + far[which].astype(jnp.float32)
        sums.append(total)
    gate, up = sums
    act = jnp.transpose(gate / (1.0 + jnp.exp(-gate)) * up)
    samples, rows, _ = out_ref.shape
    out_ref[...] = act.reshape(samples, rows, act.shape[1]).astype(jnp.bfloat16)


def swiglu(keep, recv, fars, prev, index, samples, rows, hidden_units, block):
    cols = samples * rows
    size = keep.shape[1]
    last = keep.shape[2] // cols - 1
    own = pl.BlockSpec((2, block, cols), lambda i: (0, 0, last))
    far = pl.BlockSpec((2, block, cols), lambda i: (0, 0, 0))
    args = [keep, recv, *fars]
    specs = [own, own] + [far] * len(fars)
    aliases = {}
    if prev is not None:
        aliases = {len(args): 0}
        args.append(prev)
        specs.append(pl.BlockSpec(memory_space=pl.ANY))
    return pl.pallas_call(
        functools.partial(swiglu_kernel, len(fars)),
        grid=(1,),
        in_specs=specs,
        out_specs=pl.BlockSpec((samples, rows, block), lambda i: (0, 0, index)),
        out_shape=jax.ShapeDtypeStruct((samples, rows, hidden_units), jnp.bfloat16),
        input_output_aliases=aliases,
        compiler_params=pltpu.CompilerParams(vmem_limit_bytes=24 * MIB),
        cost_estimate=pl.CostEstimate(flops=COST, bytes_accessed=COST, transcendentals=0),
        name=f"swiglu_{index}",
    )(*args)


def body(n_mp, n_pool, hidden_states, dropout_masks, gate_weight, up_weight):
    samples, tokens, _ = dropout_masks.shape
    units = gate_weight.shape[1]
    rows = tokens // n_mp
    chips = n_mp // 2
    cols = samples * rows
    me = lax.axis_index("mp")
    chip, core = me // 2, me % 2
    offsets = list(range(1, chips)) + [0]
    dest = jnp.stack(
        [lax.rem(chip + o, chips) * 2 + (core + b) % 2 for b in (1, 0) for o in offsets]
    ).astype(jnp.int32)
    to_core = [(i, i ^ 1) for i in range(n_mp)]
    to_chip = {o: [(i, (i // 2 + o) % chips * 2 + i % 2) for i in range(n_mp)] for o in range(1, chips)}

    place = lax.axis_index("pool")[None].astype(jnp.int32)
    hiddens = [hidden_states] + [
        lax.ppermute(hidden_states, "pool", [(i, (i + d) % n_pool) for i in range(n_pool)]) for d in range(1, n_pool)
    ]
    flags = make_flags(dest, dropout_masks, n_mp)
    masked = make_masked(dest, place, flags, hiddens)
    gate_t, up_t = gate_weight.T, up_weight.T
    pad = -units % 16
    if pad:
        gate_t = jnp.pad(gate_t, ((0, pad), (0, 0)))
        up_t = jnp.pad(up_t, ((0, pad), (0, 0)))
    height = units + pad
    n_chunks = pl.cdiv(height, BLOCK)
    order = [n_chunks - 1] + list(range(n_chunks - 1))
    out = None
    waiting = []
    for index in order:
        start = index * BLOCK
        size = min(BLOCK, height - start)
        send, keep = project(masked, gate_t, up_t, start, size)
        recv = lax.ppermute(send, "mp", to_core)
        fars = []
        for i, o in enumerate(offsets[:-1]):
            cut = slice(i * cols, (i + 1) * cols)
            both = keep[:, :, cut].astype(jnp.float32) + recv[:, :, cut].astype(jnp.float32)
            both = both.astype(jnp.bfloat16)
            masked, both = lax.optimization_barrier((masked, both))
            fars.append(lax.ppermute(both, "mp", to_chip[o]))
        waiting.append((keep, recv, fars, index))
    for keep, recv, fars, index in waiting:
        out = swiglu(keep, recv, fars, out, index, samples, rows, units, BLOCK)
    return out


def solution(mesh):
    in_specs = (
        P(("groups", "pool"), "mp"),
        P(None, "groups", "mp"),
        P("mp", "pool"),
        P("mp", "pool"),
    )
    out_specs = P(None, ("groups", "mp"), "pool")
    return jax.shard_map(
        functools.partial(body, mesh.shape["mp"], mesh.shape["pool"]),
        mesh=mesh,
        in_specs=in_specs,
        out_specs=out_specs,
        check_vma=False,
    )
```

```python
import functools

import jax
import jax.numpy as jnp
from jax import lax
from jax.experimental import pallas as pl
from jax.experimental.pallas import tpu as pltpu
from jax.sharding import PartitionSpec as P

BLOCK = 640
COST = 1000
LAG = 1
VMEM_MIB = 40
FLAGS_MIB = 50
MIB = 2**20
NT = (((1,), (1,)), ((), ()))


def flags_kernel(dest_ref, masks_ref, flags_ref, raw, sems):
    n_mp, samples, rows, width = raw.shape
    blocks = [
        pltpu.make_async_copy(
            masks_ref.at[:, pl.ds(pl.multiple_of(dest_ref[r] * rows, rows), rows)], raw.at[r], sems.at[r]
        )
        for r in range(n_mp)
    ]
    for block in blocks:
        block.start()
    for r, block in enumerate(blocks):
        block.wait()
        flags = raw[r].astype(jnp.float32).astype(jnp.bfloat16)
        flags_ref[r * samples * rows : (r + 1) * samples * rows] = flags.reshape(samples * rows, width)


def make_flags(dest, masks, n_mp):
    samples, tokens, width = masks.shape
    return pl.pallas_call(
        flags_kernel,
        in_specs=[pl.BlockSpec(memory_space=pltpu.SMEM), pl.BlockSpec(memory_space=pltpu.HBM)],
        out_specs=pl.BlockSpec(memory_space=pltpu.VMEM),
        out_shape=jax.ShapeDtypeStruct((samples * tokens, width), jnp.bfloat16),
        scratch_shapes=[
            pltpu.VMEM((n_mp, samples, tokens // n_mp, width), jnp.int32),
            pltpu.SemaphoreType.DMA((n_mp,)),
        ],
        compiler_params=pltpu.CompilerParams(vmem_limit_bytes=FLAGS_MIB * MIB),
        cost_estimate=pl.CostEstimate(flops=COST, bytes_accessed=COST, transcendentals=0),
        name="flags",
    )(dest, masks)


def half_of(size):
    return pl.cdiv(size, 32) * 16


def load(start, size, gate_ref, up_ref, weights_ref, sems):
    bounds = (0, half_of(size), size)
    copies = []
    for piece in range(2):
        low, n = bounds[piece], bounds[piece + 1] - bounds[piece]
        for which, ref in enumerate((gate_ref, up_ref)):
            if n:
                copy = pltpu.make_async_copy(
                    ref.at[pl.ds(start + low, n)], weights_ref.at[which, pl.ds(low, n)], sems.at[which, piece]
                )
                copy.start()
                copies.append(copy)
    return copies


def multiply(part, weights_ref, masked_ref, out_refs):
    far_gate, far_up, near, keep_far, keep_near = out_refs
    far = far_gate.shape[1]
    half = masked_ref.shape[0] // 2
    for which, send_far in enumerate((far_gate, far_up)):
        terms = lax.dot_general(
            weights_ref[which, part], masked_ref[...], NT, preferred_element_type=jnp.float32
        ).astype(jnp.bfloat16)
        send_far[part] = terms[:, :far]
        near[which, part] = terms[:, far:half]
        keep_far[which, part] = terms[:, half : half + far]
        keep_near[which, part] = terms[:, half + far :]


def peer(n_pool, place, d):
    return place ^ d if n_pool & (n_pool - 1) == 0 else (place + d) % n_pool


def slot_of(n_pool, place, owner):
    if n_pool & (n_pool - 1) == 0:
        return lax.bitwise_xor(place, owner)
    return lax.rem(place + n_pool - owner, n_pool)


def first_kernel(now, later, samples, n_mp, dest_ref, place_ref, gate_ref, up_ref, flags_ref, *refs):
    n_pool = len(refs) - (11 if later else 9)
    hidden_refs, refs = refs[:n_pool], refs[n_pool:]
    masked_ref, *refs = refs
    out_refs, refs = refs[:5], refs[5:]
    if later:
        later_ref, scaled, weights, sems, later_sems = refs
    else:
        scaled, weights, sems = refs
    copies = load(*now, gate_ref, up_ref, weights, sems)
    later_copies = load(*later, gate_ref, up_ref, later_ref, later_sems) if later else []
    piece = scaled.shape[1]
    rows = flags_ref.shape[0] // (n_mp * samples)
    for d in range(n_pool):
        scaled[d] = hidden_refs[d][...].astype(jnp.float32) * (1.0 / 0.9)
    step = min(rows, piece)

    @pl.loop(0, n_mp)
    def _(r):
        for low in range(0, rows, step):
            token = dest_ref[r] * rows + low
            slot = slot_of(n_pool, place_ref[0], lax.div(token, piece))
            inside = pl.multiple_of(lax.rem(token, piece), step)
            part = scaled[slot, pl.ds(inside, step)]
            for m in range(samples):
                at = pl.ds(pl.multiple_of((r * samples + m) * rows + low, step), step)
                masked_ref[at] = (part * flags_ref[at].astype(jnp.float32)).astype(jnp.bfloat16)

    size = now[1]
    low = 0
    while copies:
        pair, copies = copies[:2], copies[2:]
        for copy in pair:
            copy.wait()
        high = half_of(size) if copies else size
        multiply(slice(low, high), weights, masked_ref, out_refs)
        low = high
    for copy in later_copies:
        copy.wait()


def product_shapes(rows, size, cols):
    far = rows // 2 - cols
    shapes = [(size, far), (size, far), (2, size, cols), (2, size, far), (2, size, cols)]
    return [jax.ShapeDtypeStruct(shape, jnp.bfloat16) for shape in shapes]


def project_first(dest, place, gate_t, up_t, flags, hiddens, now, later, samples, n_mp, cols):
    rows, width = flags.shape
    smem = pl.BlockSpec(memory_space=pltpu.SMEM)
    vmem = pl.BlockSpec(memory_space=pltpu.VMEM)
    hbm = pl.BlockSpec(memory_space=pltpu.HBM)
    shapes = [jax.ShapeDtypeStruct((rows, width), jnp.bfloat16)] + product_shapes(rows, now[1], cols)
    scratch = [
        pltpu.VMEM((len(hiddens), *hiddens[0].shape), jnp.float32),
        pltpu.VMEM((2, now[1], width), jnp.bfloat16),
        pltpu.SemaphoreType.DMA((2, 2)),
    ]
    if later:
        shapes.append(jax.ShapeDtypeStruct((2, later[1], width), jnp.bfloat16))
        scratch.append(pltpu.SemaphoreType.DMA((2, 2)))
    return pl.pallas_call(
        functools.partial(first_kernel, now, later, samples, n_mp),
        in_specs=[smem, smem, hbm, hbm] + [vmem] * (1 + len(hiddens)),
        out_specs=[vmem] * len(shapes),
        out_shape=shapes,
        scratch_shapes=scratch,
        compiler_params=pltpu.CompilerParams(vmem_limit_bytes=VMEM_MIB * MIB),
        cost_estimate=pl.CostEstimate(flops=COST, bytes_accessed=COST, transcendentals=0),
        name="project_first",
    )(dest, place, gate_t, up_t, flags, *hiddens)


def project_kernel(later, masked_ref, weights_ref, gate_ref, up_ref, *refs):
    out_refs, rest = refs[:5], refs[5:]
    copies = load(*later, gate_ref, up_ref, *rest) if later else []
    size = weights_ref.shape[1]
    step = half_of(size)

    @pl.loop(0, 2)
    def _(i):
        multiply(pl.ds(pl.multiple_of(i * (size - step), 16), step), weights_ref, masked_ref, out_refs)

    for copy in copies:
        copy.wait()


def project(masked, weights, gate_t, up_t, later, cols):
    rows, width = masked.shape
    size = weights.shape[1]
    shapes = product_shapes(rows, size, cols)
    scratch = []
    if later:
        shapes.append(jax.ShapeDtypeStruct((2, later[1], width), jnp.bfloat16))
        scratch.append(pltpu.SemaphoreType.DMA((2, 2)))
    vmem = pl.BlockSpec(memory_space=pltpu.VMEM)
    hbm = pl.BlockSpec(memory_space=pltpu.HBM)
    return pl.pallas_call(
        functools.partial(project_kernel, later),
        in_specs=[vmem, vmem, hbm, hbm],
        out_specs=[vmem] * len(shapes),
        out_shape=shapes,
        scratch_shapes=scratch,
        compiler_params=pltpu.CompilerParams(vmem_limit_bytes=VMEM_MIB * MIB),
        cost_estimate=pl.CostEstimate(flops=COST, bytes_accessed=COST, transcendentals=0),
        name=f"project_{size}",
    )(masked, weights, gate_t, up_t)


def add_kernel(keep_ref, gate_ref, up_ref, *outs):
    cols = outs[0].shape[2]
    for which, ref in enumerate((gate_ref, up_ref)):
        for i, out in enumerate(outs):
            cut = slice(i * cols, (i + 1) * cols)
            total = keep_ref[which, :, cut].astype(jnp.float32) + ref[:, cut].astype(jnp.float32)
            out[which] = total.astype(jnp.bfloat16)


def add_cores(keep, gate, up, cols, name):
    _, size, far = keep.shape
    n = far // cols
    vmem = pl.BlockSpec(memory_space=pltpu.VMEM)
    return pl.pallas_call(
        add_kernel,
        in_specs=[vmem] * 3,
        out_specs=[vmem] * n,
        out_shape=[jax.ShapeDtypeStruct((2, size, cols), jnp.bfloat16)] * n,
        compiler_params=pltpu.CompilerParams(vmem_limit_bytes=16 * MIB),
        cost_estimate=pl.CostEstimate(flops=COST, bytes_accessed=COST, transcendentals=0),
        name=name,
    )(keep, gate, up)


def swiglu_kernel(n_far, *refs):
    keep_ref, recv_ref, *rest = refs
    far_refs, out_ref = rest[:n_far], rest[-1]
    sums = []
    for which in range(2):
        total = keep_ref[which].astype(jnp.float32) + recv_ref[which].astype(jnp.float32)
        for far in far_refs:
            total = total + far[which].astype(jnp.float32)
        sums.append(total)
    gate, up = sums
    act = jnp.transpose(gate / (1.0 + jnp.exp(-gate)) * up)
    samples, rows, _ = out_ref.shape
    out_ref[...] = act.reshape(samples, rows, act.shape[1]).astype(jnp.bfloat16)


def swiglu(keep, recv, fars, prev, index, samples, rows, hidden_units, block):
    cols = samples * rows
    size = keep.shape[1]
    args = [keep, recv, *fars]
    specs = [pl.BlockSpec((2, block, cols), lambda i: (0, 0, 0))] * len(args)
    aliases = {}
    if prev is not None:
        aliases = {len(args): 0}
        args.append(prev)
        specs.append(pl.BlockSpec(memory_space=pl.ANY))
    return pl.pallas_call(
        functools.partial(swiglu_kernel, len(fars)),
        grid=(1,),
        in_specs=specs,
        out_specs=pl.BlockSpec((samples, rows, block), lambda i: (0, 0, index)),
        out_shape=jax.ShapeDtypeStruct((samples, rows, hidden_units), jnp.bfloat16),
        input_output_aliases=aliases,
        compiler_params=pltpu.CompilerParams(vmem_limit_bytes=24 * MIB),
        cost_estimate=pl.CostEstimate(flops=COST, bytes_accessed=COST, transcendentals=0),
        name=f"swiglu_{index}",
    )(*args)


def body(n_mp, n_pool, hidden_states, dropout_masks, gate_weight, up_weight):
    samples, tokens, _ = dropout_masks.shape
    units = gate_weight.shape[1]
    rows = tokens // n_mp
    chips = n_mp // 2
    cols = samples * rows
    me = lax.axis_index("mp")
    chip, core = me // 2, me % 2
    offsets = list(range(1, chips)) + [0]
    dest = jnp.stack(
        [lax.rem(chip + o, chips) * 2 + (core + b) % 2 for b in (1, 0) for o in offsets]
    ).astype(jnp.int32)
    to_core = [(i, i ^ 1) for i in range(n_mp)]
    to_chip = {o: [(i, (i // 2 + o) % chips * 2 + i % 2) for i in range(n_mp)] for o in range(1, chips)}

    place = lax.axis_index("pool")[None].astype(jnp.int32)
    hiddens = [hidden_states] + [
        lax.ppermute(hidden_states, "pool", [(i, peer(n_pool, i, d)) for i in range(n_pool)]) for d in range(1, n_pool)
    ]
    gate_t, up_t = gate_weight.T, up_weight.T
    pad = -units % 16
    if pad:
        gate_t = jnp.pad(gate_t, ((0, pad), (0, 0)))
        up_t = jnp.pad(up_t, ((0, pad), (0, 0)))
    height = units + pad
    n_chunks = pl.cdiv(height, BLOCK)
    order = [n_chunks - 1] + list(range(n_chunks - 1))
    spans = [(index * BLOCK, min(BLOCK, height - index * BLOCK)) for index in order]
    flags = make_flags(dest, dropout_masks, n_mp)
    out = None
    waiting = []
    for i, index in enumerate(order):
        start = spans[i][0]
        later = spans[i + 1] if i + 1 < n_chunks else None
        if i == 0:
            masked, *products = project_first(
                dest, place, gate_t, up_t, flags, hiddens, spans[0], later, samples, n_mp, cols
            )
        else:
            products = project(masked, weights, gate_t, up_t, later, cols)
        far_gate, far_up, near, keep_far, keep_near, *weights = products
        weights = weights[0] if weights else None
        far_gate = lax.ppermute(far_gate, "mp", to_core)
        far_up = lax.ppermute(far_up, "mp", to_core)
        if waiting and later is None:
            near, waiting[-1][2] = lax.optimization_barrier((near, waiting[-1][2]))
        near = lax.ppermute(near, "mp", to_core)
        sums = add_cores(keep_far, far_gate, far_up, cols, f"add_{start}")
        masked, sums = lax.optimization_barrier((masked, sums))
        fars = [lax.ppermute(total, "mp", to_chip[o]) for total, o in zip(sums, offsets)]
        waiting.append([keep_near, near, fars, index])
        if len(waiting) > LAG:
            old = waiting[-1 - LAG]
            masked, old[2] = lax.optimization_barrier((masked, old[2]))
    for keep, recv, fars, index in waiting:
        out = swiglu(keep, recv, fars, out, index, samples, rows, units, BLOCK)
    return out


def solution(mesh):
    in_specs = (
        P(("groups", "pool"), "mp"),
        P(None, "groups", "mp"),
        P("mp", "pool"),
        P("mp", "pool"),
    )
    out_specs = P(None, ("groups", "mp"), "pool")
    return jax.shard_map(
        functools.partial(body, mesh.shape["mp"], mesh.shape["pool"]),
        mesh=mesh,
        in_specs=in_specs,
        out_specs=out_specs,
        check_vma=False,
    )
```
